128 devices in a mesh: row: 32 (over x, y, core), col: 4 (over z).
Axes of the slice: x: 4, y: 4, z: 4, core: 2. Of those that a mesh axis runs over, the one named last changes fastest.
Arguments:
- design: float32 [256, 1048576], P('col', 'row'), may hold values from -6 to 6
- sign_bits: int32 [1048576], P('row'), may hold values from 0 to 1
- picks: int32 [2048], replicated, may hold values from 0 to 1048575
- owners: int32 [2048, 1], replicated, may hold values from 0 to 31; in each aligned block of 2048 rows (0 to 2047, 2048 to 4095, ...) at most 128 rows name the same one
Outputs:
- sketch: float32 [256, 4096], P('col', 'row')
The draws below stay inside these ranges and needn't reach their ends.
Inputs may be any that keep to these rules, and one draw needn't show every extreme that they name: `owners`: no owner is named by more than 128 samples, a bound that some block reaches.
All inputs are finite; a program needn't handle non-finite values.
Results may differ from the reference program's by a relative error of at most 0.000071.
Values sent between devices are 32-bit elements; how exact they have to be, the bound alone decides.
No kernel may reach another device: no remote copies, remote signals or barrier semaphores. Data moves between devices by JAX's collectives and lax.ppermute only.
A program may use at most 128 MiB of HBM per device.

```python
import math
import jax
import jax.numpy as jnp
import numpy as np
from jax import lax

COLS = 256
ROWS = 1048576
SAMPLES = 2048
CAP = 128
SLOTS = 4096
N_ROW = 32


def touch_ends(values, key, least, largest):
    place = [jax.random.randint(jax.random.fold_in(key, axis), (), 0, length) for axis, length in enumerate(values.shape)]
    widest = values.shape.index(max(values.shape))
    next_to = place[:widest] + [(place[widest] + 1) % values.shape[widest]] + place[widest + 1:]
    return values.at[tuple(place)].set(least).at[tuple(next_to)].set(largest)


def steps_of(key, dims, pieces, low, top_value):
    def one(axis_at, blocks):
        draws = jax.random.uniform(jax.random.fold_in(jax.random.fold_in(key, 6), axis_at), (blocks,), jnp.float32, low / len(pieces), top_value / len(pieces))
        return jnp.repeat(jnp.exp(draws), dims[axis_at] // blocks).reshape((-1,) + (1,) * (len(dims) - axis_at - 1))

    loudness = one(*pieces[0])
    for cut in pieces[1:]:
        loudness = loudness * one(*cut)
    return loudness


def shared_out(key, own, number, rows, amount, top, bound, skew):
    order = jax.random.permutation(key, amount)
    crowded, usual = load_shares(amount, rows * top, bound, skew, True), load_shares(amount, rows * top, bound, skew, False)
    places = jnp.arange(amount)

    def named(sizes, turn):
        used = int((sizes > 0).sum())
        fixed = max(1, used // 4)
        shifted = fixed + (places - fixed + turn * (used - fixed)) % max(1, amount - fixed)
        return jnp.zeros((amount,), jnp.int32).at[order[jnp.where(places < fixed, places, shifted)]].set(jnp.asarray(sizes, jnp.int32))

    sizes = jnp.where(number % 4 == 0, named(crowded, number // 4), named(usual, number - number // 4 - 1))
    mixed = jax.random.permutation(jax.random.fold_in(own, 3), amount)
    donor, receiver = mixed[0:amount // 2 * 2:2], mixed[1:amount // 2 * 2:2]
    margin = jnp.minimum(sizes[donor] - 1, bound - sizes[receiver]) // 2
    margin = jnp.where((donor == order[0]) | (receiver == order[0]) | (sizes[receiver] == 0), 0, jnp.maximum(margin, 0))
    shifted = jax.random.randint(jax.random.fold_in(own, 4), (amount // 2,), 0, 1 << 20) % (margin + 1)
    sizes = sizes.at[donor].add(-shifted).at[receiver].add(shifted)
    members = jnp.searchsorted(jnp.cumsum(sizes), jnp.arange(rows * top), side="right").astype(jnp.int32)
    listing = members.reshape(top, rows).T
    listing = listing[jax.random.permutation(jax.random.fold_in(own, 1), rows)]
    turn = jax.random.randint(jax.random.fold_in(own, 2), (rows, 1), 0, top)
    return jnp.take_along_axis(listing, (jnp.arange(top)[None, :] + turn) % top, axis=1)


def load_shares(amount, total, reach, skew, full):
    portions = [(1 << 20) // math.isqrt(grade ** skew) + 1 for grade in range(1, amount + 1)]
    largest = reach if full else min(reach, max(-(-total // amount), total * portions[0] // sum(portions)))
    least = 1 if total - largest >= amount - 1 else 0
    counts, spare = [largest] + [least] * (amount - 1), total - largest - least * (amount - 1)
    while spare > 0:
        movable = [i for i in range(1, amount) if counts[i] < largest] or [i for i in range(1, amount) if counts[i] < reach]
        mass, budget = sum([portions[i] for i in movable]), spare
        for i in movable:
            addition = min(reach - counts[i], max(1, budget * portions[i] // mass), spare)
            counts[i] = counts[i] + addition
            spare = spare - addition
    return np.array(counts)


def normal_values(stream_key, extent, spread, bound, pieces=(), kind=jnp.bfloat16):
    entries = jax.random.normal(stream_key, extent, jnp.float32) * spread
    if len(pieces) > 0:
        entries = steps_of(stream_key, extent, pieces, -0.22, 0.18) * entries
    return jnp.clip(entries, min=-bound, max=bound).astype(kind)


def setup_inputs(seed: int = 0) -> dict:
    streams_of = jax.random.split(jax.random.key(seed), 5)
    design = normal_values(streams_of[0], (COLS, ROWS), 1.0, 6.0, ((0, 4), (1, 32)), jnp.float32)
    sign_bits = touch_ends(jax.random.randint(streams_of[1], (ROWS,), 0, 2), jax.random.fold_in(streams_of[1], 1), 0, 1).astype(jnp.int32)
    picks = touch_ends(jax.random.randint(streams_of[2], (SAMPLES,), 0, ROWS), jax.random.fold_in(streams_of[2], 1), 0, ROWS - 1).astype(jnp.int32)
    owners_keys = jax.random.split(jax.random.fold_in(streams_of[3], 1), SAMPLES // SAMPLES)
    owners_turns = jax.random.permutation(jax.random.fold_in(streams_of[3], 3), SAMPLES // SAMPLES)
    owners = jax.vmap(lambda own, number: shared_out(jax.random.fold_in(streams_of[3], 2), own, number, SAMPLES, N_ROW, 1, CAP, 2))(owners_keys, owners_turns).reshape((SAMPLES, 1))
    return {"design": design, "sign_bits": sign_bits, "picks": picks, "owners": owners}


def walsh_block(block):
    width = block.shape[0]
    half = 1
    while half < ROWS:
        shaped = block.reshape(width, ROWS // (2 * half), 2, half)
        first = shaped[:, :, 0]
        second = shaped[:, :, 1]
        block = jnp.stack([first + second, first - second], 2).reshape(width, ROWS)
        half = half * 2
    return block

def slot_table(owners):
    owner_col = owners[:, 0]
    onehot = (owner_col[:, None] == jnp.arange(N_ROW, dtype=jnp.int32)[None, :]).astype(jnp.int32)
    before = jnp.cumsum(onehot, axis=0) - onehot
    return owner_col * CAP + lax.optimization_barrier(jnp.sum(before * onehot, axis=1))

def reference(design, sign_bits, picks, owners):
    signs = (1 - 2 * sign_bits).astype(jnp.float32)
    groups = design.reshape(COLS // 16, 16, ROWS)

    def signed_walsh(block):
        return walsh_block(block * signs[None, :])
    transformed = lax.map(signed_walsh, groups).reshape(COLS, ROWS)
    transformed = transformed * jnp.float32(1.0 / math.sqrt(ROWS))
    picked = jnp.take(transformed, picks, axis=1)
    slot = slot_table(owners)
    sketch = jnp.zeros((COLS, SLOTS), jnp.float32).at[:, slot].set(picked)
    return sketch
```

```python
import functools

import jax
import jax.numpy as jnp
from jax import lax
from jax.experimental import pallas as pl
from jax.experimental.pallas import tpu as pltpu
from jax.sharding import PartitionSpec as P

LANES = 128
SIDE_X, SIDE_Y = 4, 4
CHUNKS = 8
INNER = 16
DEPTH = 256
CAPACITY = 128
BLOCKS = 32


def parity(value, bits):
    shift = 1
    while shift < bits:
        value = value ^ (value >> shift)
        shift = shift * 2
    return value & 1


def butterflies(values):
    half = 1
    values = list(values)
    while half < len(values):
        for start in range(0, len(values), 2 * half):
            for at in range(start, start + half):
                first, second = values[at], values[at + half]
                values[at], values[at + half] = first + second, first - second
        half = half * 2
    return values


def slot_kernel(me, picks_ref, owners_ref, packed_ref, weight_ref, rows_here):
    core, along_y, along_x = me & 1, (me >> 1) & 3, me >> 3
    shape = (BLOCKS, LANES)
    target = lax.broadcasted_iota(jnp.int32, shape, 0)
    owner = owners_ref[...]
    pick = picks_ref[...]
    rel = (
        (((owner & 1) ^ core) << 4)
        | ((((owner >> 3) - along_x) & 3) << 2)
        | (((owner >> 1) - along_y) & 3)
    )
    source = pick // rows_here
    offset = pick % rows_here
    sign = (1 - 2 * parity(source & me, 8)).astype(jnp.float32)
    column = offset // DEPTH
    odd = column & 1
    row = (column >> 1) * DEPTH + (offset % DEPTH)
    groups = pick.shape[0]
    up = lax.broadcasted_iota(jnp.int32, (LANES, 2 * LANES), 0)
    to = lax.broadcasted_iota(jnp.int32, (LANES, 2 * LANES), 1)
    upper = jnp.where((to >= LANES) | (up < to), 1.0, 0.0).astype(jnp.bfloat16)
    onehot = [
        jnp.where(rel[g:g + 1, :] == target, 1.0, 0.0) for g in range(groups)
    ]
    counted = jnp.dot(
        jnp.concatenate(onehot, axis=0).astype(jnp.bfloat16),
        upper,
        preferred_element_type=jnp.float32,
    )
    base = jnp.zeros(shape, jnp.float32)
    place = lax.broadcasted_iota(jnp.int32, (CAPACITY, LANES), 0)
    total = jnp.zeros((2 * BLOCKS, LANES), jnp.float32)
    for g in range(groups):
        here = counted[g * BLOCKS:(g + 1) * BLOCKS]
        rank = jnp.sum(onehot[g] * (here[:, :LANES] + base), axis=0, keepdims=True)
        base = base + here[:, LANES:]
        rank = rank.astype(jnp.int32)
        packed_ref[g:g + 1, :] = row[g:g + 1] | ((rel[g:g + 1] * CAPACITY + rank) << 14)
        held = onehot[g] * sign[g:g + 1]
        odd_here = odd[g:g + 1].astype(jnp.float32)
        both = jnp.concatenate([held * (1.0 - odd_here), held * odd_here], axis=0)
        at = jnp.where(rank == place, 1.0, 0.0).astype(jnp.bfloat16)
        total = total + lax.dot_general(
            both.astype(jnp.bfloat16), at, (((1,), (1,)), ((), ())),
            preferred_element_type=jnp.float32,
        )
    weight_ref[...] = total * jnp.float32(2.0 ** -10)


def local_kernel(
    x_ref, bits_ref, picks_ref, owners_ref, keep_ref, send_ref,
    x_buf, signs, had, parts, table, packed, listed, weight, rows, x_sem, l_sem,
):
    width = x_ref.shape[0]
    rows_here = x_ref.shape[1]
    span = rows_here // CHUNKS
    me = lax.axis_index("row")

    def chunk_copy(g):
        return pltpu.make_async_copy(
            x_ref.at[:, pl.ds(g * span, span)], x_buf.at[g], x_sem.at[g]
        )

    for g in range(CHUNKS):
        chunk_copy(g).start()

    slot_kernel(me, picks_ref, owners_ref, packed, weight, rows_here)
    listing = pltpu.make_async_copy(packed, listed, l_sem)
    listing.start()
    signs[...] = (1 - 2 * bits_ref[...]).astype(jnp.float32)
    i = lax.broadcasted_iota(jnp.int32, (DEPTH, DEPTH), 0)
    k = lax.broadcasted_iota(jnp.int32, (DEPTH, DEPTH), 1)
    matrix = (1 - 2 * parity(i & k, 8)).astype(jnp.float32).astype(jnp.bfloat16)
    had[:, :DEPTH] = matrix
    had[:, DEPTH:] = matrix

    @pl.loop(0, CHUNKS)
    def _(g):
        chunk_copy(g).wait()
        for half in range(2):
            for c in range(0, width, 16):
                values = []
                for j in range(INNER):
                    at = j * DEPTH + half * LANES
                    sign = signs[pl.ds(g * (span // LANES) + at // LANES, 1), :]
                    values.append(x_buf[g, c:c + 16, at:at + LANES] * sign)
                for j, value in enumerate(butterflies(values)):
                    high = value.astype(jnp.bfloat16)
                    low = (value - high.astype(jnp.float32)).astype(jnp.bfloat16)
                    at = pl.ds(j * width + c, 16)
                    parts[at, half * LANES:(half + 1) * LANES] = high
                    parts[at, DEPTH + half * LANES:DEPTH + (half + 1) * LANES] = low
        for four in range(INNER // 4):
            made = lax.dot_general(
                had[...], parts[four * 4 * width:(four + 1) * 4 * width, :],
                (((1,), (1,)), ((), ())),
                preferred_element_type=jnp.float32,
            )
            at = g * (INNER // 2) + four * 2
            table[pl.ds(at * DEPTH, DEPTH), :] = made[:, :LANES]
            table[pl.ds((at + 1) * DEPTH, DEPTH), :] = made[:, LANES:]

    stretch = table.shape[0] // CHUNKS
    step = 32

    @pl.loop(0, stretch // step)
    def _(at):
        values = [table[pl.ds(g * stretch + at * step, step), :] for g in range(CHUNKS)]
        for g, value in enumerate(butterflies(values)):
            table[pl.ds(g * stretch + at * step, step), :] = value

    listing.wait()

    @pl.loop(0, packed.shape[0])
    def _(g):
        for lane in range(LANES):
            word = listed[g, lane]
            rows[pl.ds(word >> 14, 1), :] = table[pl.ds(word & 16383, 1), :]

    @pl.loop(0, BLOCKS // 2)
    def _(b):
        for out_ref, block in ((keep_ref, b), (send_ref, b + BLOCKS // 2)):
            turned = rows[pl.ds(block * CAPACITY, CAPACITY), :].T
            even = weight[pl.ds(block, 1), :]
            odd = weight[pl.ds(block + BLOCKS, 1), :]
            zero = jnp.zeros((width, CAPACITY), jnp.float32)
            value = jnp.where(even != 0.0, turned[:width] * even, zero)
            value = jnp.where(odd != 0.0, turned[width:] * odd, value)
            out_ref[b] = value


def local_parts(design, bits, picks, owners):
    width, rows_here = design.shape
    vmem = pl.BlockSpec(memory_space=pltpu.VMEM)
    half = jax.ShapeDtypeStruct((BLOCKS // 2, width, CAPACITY), jnp.float32)
    return pl.pallas_call(
        local_kernel,
        out_shape=(half, half),
        in_specs=[pl.BlockSpec(memory_space=pl.ANY), vmem, vmem, vmem],
        out_specs=(vmem, vmem),
        scratch_shapes=[
            pltpu.VMEM((CHUNKS, width, rows_here // CHUNKS), jnp.float32),
            pltpu.VMEM((rows_here // LANES, LANES), jnp.float32),
            pltpu.VMEM((DEPTH, 2 * DEPTH), jnp.bfloat16),
            pltpu.VMEM((INNER * width, 2 * DEPTH), jnp.bfloat16),
            pltpu.VMEM((rows_here // 2, LANES), jnp.float32),
            pltpu.VMEM((16, LANES), jnp.int32),
            pltpu.SMEM((16, LANES), jnp.int32),
            pltpu.VMEM((2 * BLOCKS, LANES), jnp.float32),
            pltpu.VMEM((BLOCKS * CAPACITY, LANES), jnp.float32),
            pltpu.SemaphoreType.DMA((CHUNKS,)),
            pltpu.SemaphoreType.DMA,
        ],
        compiler_params=pltpu.CompilerParams(vmem_limit_bytes=48 << 20),
    )(design, bits, picks, owners)


def place(x, y, core):
    return (x * SIDE_Y + y) * 2 + core


def shift(dx, dy, dcore):
    return [
        (place(x, y, c), place((x + dx) % SIDE_X, (y + dy) % SIDE_Y, c ^ dcore))
        for x in range(SIDE_X)
        for y in range(SIDE_Y)
        for c in range(2)
    ]


def shards(design, sign_bits, picks, owners):
    bits = sign_bits.reshape(-1, LANES)
    keep, send = local_parts(
        design, bits, picks.reshape(-1, LANES), owners.reshape(-1, LANES)
    )
    held = keep + lax.ppermute(send, "row", shift(0, 0, 1))
    own = held[0:4]
    for dx in (1, 2, 3):
        own = own + lax.ppermute(held[dx * 4:dx * 4 + 4], "row", shift(dx, 0, 0))
    out = own[0]
    for dy in (1, 2, 3):
        out = out + lax.ppermute(own[dy], "row", shift(0, dy, 0))
    return out


def solution(mesh):
    placed = (P("col", "row"), P("row"), P(), P())
    return jax.shard_map(
        shards, mesh=mesh, in_specs=placed, out_specs=P("col", "row"), check_vma=False
    )
```

```python
import functools

import jax
import jax.numpy as jnp
from jax import lax
from jax.experimental import pallas as pl
from jax.experimental.pallas import tpu as pltpu
from jax.sharding import PartitionSpec as P

LANES = 128
SIDE_X, SIDE_Y = 4, 4
CHUNKS = 8
INNER = 16
DEPTH = 256
CAPACITY = 128
BLOCKS = 32


def parity(value, bits):
    shift = 1
    while shift < bits:
        value = value ^ (value >> shift)
        shift = shift * 2
    return value & 1


def butterflies(values):
    half = 1
    values = list(values)
    while half < len(values):
        for start in range(0, len(values), 2 * half):
            for at in range(start, start + half):
                first, second = values[at], values[at + half]
                values[at], values[at + half] = first + second, first - second
        half = half * 2
    return values


def list_samples(me, picks, owners, rows_here, listed_ref, weight_ref):
    core, along_y, along_x = me & 1, (me >> 1) & 3, me >> 3
    owner_core = owners & 1
    rel_x = ((owners >> 3) - along_x) & 3
    rel_y = ((owners >> 1) - along_y) & 3
    first = jnp.where(owner_core == 0, rel_x, rel_y)
    second = jnp.where(owner_core == 0, rel_y, rel_x)
    rel = ((owner_core ^ core) << 4) | (first << 2) | second
    source = picks // rows_here
    offset = picks % rows_here
    sign = (1 - 2 * parity(source & me, 8)).astype(jnp.float32)
    column = offset // DEPTH
    odd = (column & 1).astype(jnp.float32)
    row = (column >> 1) * DEPTH + (offset % DEPTH)
    pieces = [
        sign * (1.0 - odd),
        sign * odd,
        (row & 127).astype(jnp.float32),
        (row >> 7).astype(jnp.float32),
    ]
    groups = picks.shape[0]
    up = lax.broadcasted_iota(jnp.int32, (LANES, 2 * LANES), 0)
    to = lax.broadcasted_iota(jnp.int32, (LANES, 2 * LANES), 1)
    upper = jnp.where((to >= LANES) | (up < to), 1.0, 0.0).astype(jnp.bfloat16)
    target = lax.broadcasted_iota(jnp.int32, (BLOCKS, LANES), 0)
    place = lax.broadcasted_iota(jnp.int32, (CAPACITY, LANES), 0)
    onehot = [jnp.where(rel[g:g + 1] == target, 1.0, 0.0) for g in range(groups)]
    counted = jnp.dot(
        jnp.concatenate(onehot, axis=0).astype(jnp.bfloat16),
        upper,
        preferred_element_type=jnp.float32,
    )
    base = jnp.zeros((BLOCKS, LANES), jnp.float32)
    total = jnp.zeros((len(pieces) * BLOCKS, LANES), jnp.float32)
    for g in range(groups):
        here = counted[g * BLOCKS:(g + 1) * BLOCKS]
        rank = jnp.sum(onehot[g] * (here[:, :LANES] + base), axis=0, keepdims=True)
        base = base + here[:, LANES:]
        at = jnp.where(rank.astype(jnp.int32) == place, 1.0, 0.0).astype(jnp.bfloat16)
        held = [onehot[g] * piece[g:g + 1] for piece in pieces]
        total = total + lax.dot_general(
            jnp.concatenate(held, axis=0).astype(jnp.bfloat16), at,
            (((1,), (1,)), ((), ())), preferred_element_type=jnp.float32,
        )
    weight_ref[...] = total[:2 * BLOCKS] * jnp.float32(2.0 ** -10)
    low = total[2 * BLOCKS:3 * BLOCKS].astype(jnp.int32)
    high = total[3 * BLOCKS:].astype(jnp.int32)
    listed_ref[...] = (base.astype(jnp.int32) << 16) | (high << 7) | low


def take_rows(first, blocks, table, listed, rows):
    @pl.loop(0, blocks)
    def _(b):
        count = listed[first + b, 0] >> 16

        @pl.loop(0, (count + 7) >> 3)
        def _(eight):
            for i in range(8):
                at = eight * 8 + i
                row = listed[first + b, at] & 16383
                rows[pl.ds(b * CAPACITY + at, 1), :] = table[pl.ds(row, 1), :]


def turn_rows(first, blocks, rows, weight, out_ref):
    width = out_ref.shape[1]

    @pl.loop(0, blocks // 2)
    def _(pair):
        for b in (2 * pair, 2 * pair + 1):
            turned = rows[pl.ds(b * CAPACITY, CAPACITY), :].T
            even = weight[pl.ds(first + b, 1), :]
            odd = weight[pl.ds(BLOCKS + first + b, 1), :]
            zero = jnp.zeros((width, CAPACITY), jnp.float32)
            value = jnp.where(even != 0.0, turned[:width] * even, zero)
            out_ref[b] = jnp.where(odd != 0.0, turned[width:] * odd, value)


def transform_kernel(
    x_ref, bits_ref, picks_ref, owners_ref, send_ref, table, listed_ref, weight,
    x_buf, bits, picks, owners, signs, had, parts_a, parts_b, listed, rows,
    x_sem, small_sem, l_sem,
):
    width = x_ref.shape[0]
    rows_here = x_ref.shape[1]
    span = rows_here // CHUNKS
    me = lax.axis_index("row")

    small = [
        pltpu.make_async_copy(source, to, small_sem.at[n])
        for n, (source, to) in enumerate(
            ((picks_ref, picks), (owners_ref, owners), (bits_ref, bits))
        )
    ]
    chunks = [
        pltpu.make_async_copy(
            x_ref.at[:, g * span:(g + 1) * span], x_buf.at[g], x_sem.at[g]
        )
        for g in range(CHUNKS)
    ]
    for copy in small + chunks:
        copy.start()

    i = lax.broadcasted_iota(jnp.int32, (DEPTH, DEPTH), 0)
    k = lax.broadcasted_iota(jnp.int32, (DEPTH, DEPTH), 1)
    matrix = (1 - 2 * parity(i & k, 8)).astype(jnp.float32).astype(jnp.bfloat16)
    had[:, :DEPTH] = matrix
    had[:, DEPTH:] = matrix
    small[0].wait()
    small[1].wait()
    list_samples(me, picks[...], owners[...], rows_here, listed_ref, weight)
    listing = pltpu.make_async_copy(listed_ref, listed, l_sem)
    listing.start()
    small[2].wait()
    signs[...] = (1 - 2 * bits[...]).astype(jnp.float32)

    def prepare(g, it, parts):
        c = it * 16
        for half in range(2):
            values = []
            for j in range(INNER):
                at = j * DEPTH + half * LANES
                line = (g * span + at) // LANES
                values.append(
                    x_buf[g, pl.ds(c, 16), at:at + LANES] * signs[line:line + 1, :]
                )
            for j, value in enumerate(butterflies(values)):
                high = value.astype(jnp.bfloat16)
                low = (value - high.astype(jnp.float32)).astype(jnp.bfloat16)
                at = pl.ds(j * width + c, 16)
                parts[at, half * LANES:(half + 1) * LANES] = high
                parts[at, DEPTH + half * LANES:DEPTH + (half + 1) * LANES] = low

    def multiply(g, it, parts):
        made = lax.dot_general(
            had[...], parts[pl.ds(it * 4 * width, 4 * width), :],
            (((1,), (1,)), ((), ())), preferred_element_type=jnp.float32,
        )
        at = (g * (INNER // 2) + it * 2) * DEPTH
        table[pl.ds(at, DEPTH), :] = made[:, :LANES]
        table[pl.ds(at + DEPTH, DEPTH), :] = made[:, LANES:]

    both = (parts_a, parts_b)
    for g in range(CHUNKS + 1):
        if g < CHUNKS:
            chunks[g].wait()

        @pl.loop(0, 4)
        def _(it):
            if g > 0:
                multiply(g - 1, it, both[(g - 1) % 2])
            if g < CHUNKS:
                prepare(g, it, both[g % 2])

    stretch = table.shape[0] // CHUNKS
    step = 32

    @pl.loop(0, stretch // step)
    def _(at):
        values = [table[pl.ds(g * stretch + at * step, step), :] for g in range(CHUNKS)]
        for g, value in enumerate(butterflies(values)):
            table[pl.ds(g * stretch + at * step, step), :] = value

    listing.wait()
    take_rows(BLOCKS // 2, BLOCKS // 2, table, listed, rows)
    turn_rows(BLOCKS // 2, BLOCKS // 2, rows, weight, send_ref)


def take_kernel(first, table, listed_ref, weight, out_ref, listed, rows, l_sem):
    listing = pltpu.make_async_copy(listed_ref, listed, l_sem)
    listing.start()
    listing.wait()
    blocks = out_ref.shape[0]
    take_rows(first, blocks, table, listed, rows)
    turn_rows(first, blocks, rows, weight, out_ref)


VMEM = pl.BlockSpec(memory_space=pltpu.VMEM)
ANY = pl.BlockSpec(memory_space=pltpu.HBM)


def transform(design, bits, picks, owners):
    width, rows_here = design.shape
    f32, i32 = jnp.float32, jnp.int32
    return pl.pallas_call(
        transform_kernel,
        out_shape=(
            jax.ShapeDtypeStruct((BLOCKS // 2, width, CAPACITY), f32),
            jax.ShapeDtypeStruct((rows_here // 2, LANES), f32),
            jax.ShapeDtypeStruct((BLOCKS, LANES), i32),
            jax.ShapeDtypeStruct((2 * BLOCKS, LANES), f32),
        ),
        in_specs=[ANY] * 4,
        out_specs=(VMEM,) * 4,
        scratch_shapes=[
            pltpu.VMEM((CHUNKS, width, rows_here // CHUNKS), f32),
            pltpu.VMEM(bits.shape, i32),
            pltpu.VMEM(picks.shape, i32),
            pltpu.VMEM(owners.shape, i32),
            pltpu.VMEM(bits.shape, f32),
            pltpu.VMEM((DEPTH, 2 * DEPTH), jnp.bfloat16),
            pltpu.VMEM((INNER * width, 2 * DEPTH), jnp.bfloat16),
            pltpu.VMEM((INNER * width, 2 * DEPTH), jnp.bfloat16),
            pltpu.SMEM((BLOCKS, LANES), i32),
            pltpu.VMEM((BLOCKS // 2 * CAPACITY, LANES), f32),
            pltpu.SemaphoreType.DMA((CHUNKS,)),
            pltpu.SemaphoreType.DMA((3,)),
            pltpu.SemaphoreType.DMA,
        ],
        compiler_params=pltpu.CompilerParams(vmem_limit_bytes=24 << 20),
    )(*[
        pltpu.with_memory_space_constraint(a, pltpu.HBM)
        for a in (design, bits, picks, owners)
    ])


def take(first, blocks, width, table, listed, weight):
    return pl.pallas_call(
        functools.partial(take_kernel, first),
        out_shape=jax.ShapeDtypeStruct((blocks, width, CAPACITY), jnp.float32),
        in_specs=[VMEM] * 3,
        out_specs=VMEM,
        scratch_shapes=[
            pltpu.SMEM((BLOCKS, LANES), jnp.int32),
            pltpu.VMEM((blocks * CAPACITY, LANES), jnp.float32),
            pltpu.SemaphoreType.DMA,
        ],
        compiler_params=pltpu.CompilerParams(vmem_limit_bytes=24 << 20),
        cost_estimate=pl.CostEstimate(
            flops=0, bytes_accessed=blocks << 18, transcendentals=0
        ),
    )(table, listed, weight)


def place(x, y, core):
    return (x * SIDE_Y + y) * 2 + core


def core_swap():
    return [(i, i ^ 1) for i in range(BLOCKS)]


def shift(step, first):
    pairs = []
    for x in range(SIDE_X):
        for y in range(SIDE_Y):
            for core in range(2):
                if (core == 0) == first:
                    to = place((x + step) % SIDE_X, y, core)
                else:
                    to = place(x, (y + step) % SIDE_Y, core)
                pairs.append((place(x, y, core), to))
    return pairs


def shards(design, sign_bits, picks, owners):
    width = design.shape[0]
    send, *made = transform(
        design,
        sign_bits.reshape(-1, LANES),
        picks.reshape(-1, LANES),
        owners.reshape(-1, LANES),
    )
    held = lax.ppermute(send, "row", core_swap())
    held = take(0, BLOCKS // 2, width, *made) + held
    own = held[0:4]
    for step in (1, 2, 3):
        own = own + lax.ppermute(held[step * 4:step * 4 + 4], "row", shift(step, True))
    out = own[0]
    for step in (1, 2, 3):
        out = out + lax.ppermute(own[step], "row", shift(step, False))
    return out


def solution(mesh):
    placed = (P("col", "row"), P("row"), P(), P())
    return jax.shard_map(
        shards, mesh=mesh, in_specs=placed, out_specs=P("col", "row"), check_vma=False
    )
```

```python
import functools

import jax
import jax.numpy as jnp
from jax import lax
from jax.experimental import pallas as pl
from jax.experimental.pallas import tpu as pltpu
from jax.sharding import PartitionSpec as P

LANES = 128
SIDE_X, SIDE_Y = 4, 4
CHUNKS = 8
INNER = 16
DEPTH = 256
CAPACITY = 128
STEP = 32
AHEAD = 3
BLOCKS = 32


def parity(value, bits):
    shift = 1
    while shift < bits:
        value = value ^ (value >> shift)
        shift = shift * 2
    return value & 1


def butterflies(values):
    half = 1
    values = list(values)
    while half < len(values):
        for start in range(0, len(values), 2 * half):
            for at in range(start, start + half):
                first, second = values[at], values[at + half]
                values[at], values[at + half] = first + second, first - second
        half = half * 2
    return values


def list_samples(me, picks, owners, rows_here, listed_ref, weight_ref):
    core, along_y, along_x = me & 1, (me >> 1) & 3, me >> 3
    owner_core = owners & 1
    rel_x = ((owners >> 3) - along_x) & 3
    rel_y = ((owners >> 1) - along_y) & 3
    first = jnp.where(owner_core == 0, rel_x, rel_y)
    second = jnp.where(owner_core == 0, rel_y, rel_x)
    rel = ((owner_core ^ core) << 4) | (first << 2) | second
    source = picks // rows_here
    offset = picks % rows_here
    sign = (1 - 2 * parity(source & me, 8)).astype(jnp.float32)
    column = offset // DEPTH
    odd = (column & 1).astype(jnp.float32)
    row = (column >> 1) * DEPTH + (offset % DEPTH)
    pieces = [
        sign * (1.0 - odd),
        sign * odd,
        (row & 127).astype(jnp.float32),
        (row >> 7).astype(jnp.float32),
    ]
    groups = picks.shape[0]
    up = lax.broadcasted_iota(jnp.int32, (LANES, 2 * LANES), 0)
    to = lax.broadcasted_iota(jnp.int32, (LANES, 2 * LANES), 1)
    upper = jnp.where((to >= LANES) | (up < to), 1.0, 0.0).astype(jnp.bfloat16)
    target = lax.broadcasted_iota(jnp.int32, (BLOCKS, LANES), 0)
    place = lax.broadcasted_iota(jnp.int32, (CAPACITY, LANES), 0)
    onehot = [jnp.where(rel[g:g + 1] == target, 1.0, 0.0) for g in range(groups)]
    counted = jnp.dot(
        jnp.concatenate(onehot, axis=0).astype(jnp.bfloat16),
        upper,
        preferred_element_type=jnp.float32,
    )
    base = jnp.zeros((BLOCKS, LANES), jnp.float32)
    total = jnp.zeros((len(pieces) * BLOCKS, LANES), jnp.float32)
    for g in range(groups):
        here = counted[g * BLOCKS:(g + 1) * BLOCKS]
        rank = jnp.sum(onehot[g] * (here[:, :LANES] + base), axis=0, keepdims=True)
        base = base + here[:, LANES:]
        at = jnp.where(rank.astype(jnp.int32) == place, 1.0, 0.0).astype(jnp.bfloat16)
        held = [onehot[g] * piece[g:g + 1] for piece in pieces]
        total = total + lax.dot_general(
            jnp.concatenate(held, axis=0).astype(jnp.bfloat16), at,
            (((1,), (1,)), ((), ())), preferred_element_type=jnp.float32,
        )
    weight_ref[...] = total[:2 * BLOCKS] * jnp.float32(2.0 ** -10)
    low = total[2 * BLOCKS:3 * BLOCKS].astype(jnp.int32)
    high = total[3 * BLOCKS:].astype(jnp.int32)
    listed_ref[:BLOCKS] = (high << 7) | low
    listed_ref[BLOCKS:] = base.astype(jnp.int32)


def take_rows(first, blocks, table, listed, rows):
    @pl.loop(0, blocks)
    def _(b):
        count = listed[BLOCKS + first + b, 0]
        for start in range(0, CAPACITY, STEP):
            @pl.when(count > start)
            def _():
                for at in range(start, start + STEP):
                    row = listed[first + b, at]
                    rows[pl.ds(b * CAPACITY + at, 1), :] = table[pl.ds(row, 1), :]


def turn_rows(first, blocks, rows, weight, out_ref):
    width = out_ref.shape[1]

    @pl.loop(0, blocks // 2)
    def _(pair):
        for b in (2 * pair, 2 * pair + 1):
            turned = rows[pl.ds(b * CAPACITY, CAPACITY), :].T
            even = weight[pl.ds(first + b, 1), :]
            odd = weight[pl.ds(BLOCKS + first + b, 1), :]
            zero = jnp.zeros((width, CAPACITY), jnp.float32)
            value = jnp.where(even != 0.0, turned[:width] * even, zero)
            out_ref[b] = jnp.where(odd != 0.0, turned[width:] * odd, value)


def transform_kernel(
    x_ref, bits_ref, picks_ref, owners_ref, send_ref, table, listed_ref, weight,
    x_buf, bits, picks, owners, signs, had, parts_a, parts_b, listed, rows,
    x_sem, small_sem, l_sem,
):
    width = x_ref.shape[0]
    rows_here = x_ref.shape[1]
    span = rows_here // CHUNKS
    me = lax.axis_index("row")

    small = [
        pltpu.make_async_copy(source, to, small_sem.at[n])
        for n, (source, to) in enumerate(
            ((picks_ref, picks), (owners_ref, owners), (bits_ref, bits))
        )
    ]
    def chunk(g):
        at = pl.multiple_of(g * span, span)
        return pltpu.make_async_copy(
            x_ref.at[:, pl.ds(at, span)], x_buf.at[g], x_sem.at[g]
        )

    for copy in small:
        copy.start()
    for g in range(AHEAD):
        chunk(g).start()

    i = lax.broadcasted_iota(jnp.int32, (DEPTH, DEPTH), 0)
    k = lax.broadcasted_iota(jnp.int32, (DEPTH, DEPTH), 1)
    matrix = (1 - 2 * parity(i & k, 8)).astype(jnp.float32).astype(jnp.bfloat16)
    had[:, :DEPTH] = matrix
    had[:, DEPTH:] = matrix
    small[0].wait()
    small[1].wait()
    list_samples(me, picks[...], owners[...], rows_here, listed_ref, weight)
    listing = pltpu.make_async_copy(listed_ref, listed, l_sem)
    listing.start()
    small[2].wait()
    signs[...] = (1 - 2 * bits[...]).astype(jnp.float32)

    def prepare(g, c, half, parts):
        values = []
        for j in range(INNER):
            at = j * DEPTH + half * LANES
            sign = signs[pl.ds(g * (span // LANES) + at // LANES, 1), :]
            values.append(x_buf[g, c:c + 16, at:at + LANES] * sign)
        for j, value in enumerate(butterflies(values)):
            high = value.astype(jnp.bfloat16)
            low = (value - high.astype(jnp.float32)).astype(jnp.bfloat16)
            at = slice(j * width + c, j * width + c + 16)
            parts[at, half * LANES:(half + 1) * LANES] = high
            parts[at, DEPTH + half * LANES:DEPTH + (half + 1) * LANES] = low

    def multiply(g, four, parts):
        made = lax.dot_general(
            had[...], parts[four * 4 * width:(four + 1) * 4 * width, :],
            (((1,), (1,)), ((), ())), preferred_element_type=jnp.float32,
        )
        at = (g * (INNER // 2) + four * 2) * DEPTH
        table[pl.ds(at, DEPTH), :] = made[:, :LANES]
        table[pl.ds(at + DEPTH, DEPTH), :] = made[:, LANES:]

    def stage(g, before, after):
        for four in range(4):
            if before is not None:
                multiply(g - 1, four, before)
            if after is not None:
                prepare(g, four * 16, 0, after)
                prepare(g, four * 16, 1, after)

    def wait(g):
        chunk(g).wait()

        @pl.when(g + AHEAD < CHUNKS)
        def _():
            chunk(g + AHEAD).start()

    wait(0)
    stage(0, None, parts_a)

    @pl.loop(0, CHUNKS // 2 - 1)
    def _(pair):
        wait(2 * pair + 1)
        stage(2 * pair + 1, parts_a, parts_b)
        wait(2 * pair + 2)
        stage(2 * pair + 2, parts_b, parts_a)

    wait(CHUNKS - 1)

    @pl.when(me < BLOCKS)
    def _():
        stage(CHUNKS - 1, parts_a, parts_b)

    @pl.when(me < BLOCKS)
    def _():
        stage(CHUNKS, parts_b, None)


    stretch = table.shape[0] // CHUNKS
    step = 32

    @pl.loop(0, stretch // step)
    def _(at):
        values = [table[pl.ds(g * stretch + at * step, step), :] for g in range(CHUNKS)]
        for g, value in enumerate(butterflies(values)):
            table[pl.ds(g * stretch + at * step, step), :] = value

    listing.wait()
    take_rows(BLOCKS // 2, BLOCKS // 2, table, listed, rows)
    turn_rows(BLOCKS // 2, BLOCKS // 2, rows, weight, send_ref)


def take_kernel(first, table, listed_ref, weight, out_ref, listed, rows, l_sem):
    listing = pltpu.make_async_copy(listed_ref, listed, l_sem)
    listing.start()
    listing.wait()
    blocks = out_ref.shape[0]
    take_rows(first, blocks, table, listed, rows)
    turn_rows(first, blocks, rows, weight, out_ref)


VMEM = pl.BlockSpec(memory_space=pltpu.VMEM)
ANY = pl.BlockSpec(memory_space=pltpu.HBM)


def transform(design, bits, picks, owners):
    width, rows_here = design.shape
    f32, i32 = jnp.float32, jnp.int32
    return pl.pallas_call(
        transform_kernel,
        out_shape=(
            jax.ShapeDtypeStruct((BLOCKS // 2, width, CAPACITY), f32),
            jax.ShapeDtypeStruct((rows_here // 2, LANES), f32),
            jax.ShapeDtypeStruct((2 * BLOCKS, LANES), i32),
            jax.ShapeDtypeStruct((2 * BLOCKS, LANES), f32),
        ),
        in_specs=[ANY] * 4,
        out_specs=(VMEM,) * 4,
        scratch_shapes=[
            pltpu.VMEM((CHUNKS, width, rows_here // CHUNKS), f32),
            pltpu.VMEM(bits.shape, i32),
            pltpu.VMEM(picks.shape, i32),
            pltpu.VMEM(owners.shape, i32),
            pltpu.VMEM(bits.shape, f32),
            pltpu.VMEM((DEPTH, 2 * DEPTH), jnp.bfloat16),
            pltpu.VMEM((INNER * width, 2 * DEPTH), jnp.bfloat16),
            pltpu.VMEM((INNER * width, 2 * DEPTH), jnp.bfloat16),
            pltpu.SMEM((2 * BLOCKS, LANES), i32),
            pltpu.VMEM((BLOCKS // 2 * CAPACITY, LANES), f32),
            pltpu.SemaphoreType.DMA((CHUNKS,)),
            pltpu.SemaphoreType.DMA((3,)),
            pltpu.SemaphoreType.DMA,
        ],
        compiler_params=pltpu.CompilerParams(vmem_limit_bytes=24 << 20),
    )(*[
        pltpu.with_memory_space_constraint(a, pltpu.HBM)
        for a in (design, bits, picks, owners)
    ])


def take(first, blocks, width, table, listed, weight):
    return pl.pallas_call(
        functools.partial(take_kernel, first),
        out_shape=jax.ShapeDtypeStruct((blocks, width, CAPACITY), jnp.float32),
        in_specs=[VMEM] * 3,
        out_specs=VMEM,
        scratch_shapes=[
            pltpu.SMEM((2 * BLOCKS, LANES), jnp.int32),
            pltpu.VMEM((blocks * CAPACITY, LANES), jnp.float32),
            pltpu.SemaphoreType.DMA,
        ],
        compiler_params=pltpu.CompilerParams(vmem_limit_bytes=24 << 20),
        cost_estimate=pl.CostEstimate(
            flops=0, bytes_accessed=blocks << 18, transcendentals=0
        ),
    )(table, listed, weight)


def place(x, y, core):
    return (x * SIDE_Y + y) * 2 + core


def core_swap():
    return [(i, i ^ 1) for i in range(BLOCKS)]


def shift(step, first):
    pairs = []
    for x in range(SIDE_X):
        for y in range(SIDE_Y):
            for core in range(2):
                if (core == 0) == first:
                    to = place((x + step) % SIDE_X, y, core)
                else:
                    to = place(x, (y + step) % SIDE_Y, core)
                pairs.append((place(x, y, core), to))
    return pairs


def shards(design, sign_bits, picks, owners):
    width = design.shape[0]
    send, *made = transform(
        design,
        sign_bits.reshape(-1, LANES),
        picks.reshape(-1, LANES),
        owners.reshape(-1, LANES),
    )
    held = lax.ppermute(send, "row", core_swap())
    held = take(0, BLOCKS // 2, width, *made) + held
    own = held[0:4]
    for step in (1, 2, 3):
        own = own + lax.ppermute(held[step * 4:step * 4 + 4], "row", shift(step, True))
    out = own[0]
    for step in (1, 2, 3):
        out = out + lax.ppermute(own[step], "row", shift(step, False))
    return out


def solution(mesh):
    placed = (P("col", "row"), P("row"), P(), P())
    return jax.shard_map(
        shards, mesh=mesh, in_specs=placed, out_specs=P("col", "row"), check_vma=False
    )
```

```python
import functools

import jax
import jax.numpy as jnp
from jax import lax
from jax.experimental import pallas as pl
from jax.experimental.pallas import tpu as pltpu
from jax.sharding import PartitionSpec as P

LANES = 128
SIDE_X, SIDE_Y = 4, 4
CHUNKS = 8
INNER = 16
DEPTH = 256
CAPACITY = 128
STEP = 32
AHEAD = 3
BLOCKS = 32


def parity(value, bits):
    shift = 1
    while shift < bits:
        value = value ^ (value >> shift)
        shift = shift * 2
    return value & 1


def butterflies(values):
    half = 1
    values = list(values)
    while half < len(values):
        for start in range(0, len(values), 2 * half):
            for at in range(start, start + half):
                first, second = values[at], values[at + half]
                values[at], values[at + half] = first + second, first - second
        half = half * 2
    return values


def list_samples(me, picks, owners, rows_here, listed_ref, weight_ref):
    core, along_y, along_x = me & 1, (me >> 1) & 3, me >> 3
    owner_core = owners & 1
    rel_x = ((owners >> 3) - along_x) & 3
    rel_y = ((owners >> 1) - along_y) & 3
    first = jnp.where(owner_core == 0, rel_x, rel_y)
    second = jnp.where(owner_core == 0, rel_y, rel_x)
    rel = ((owner_core ^ core) << 4) | (first << 2) | second
    source = picks // rows_here
    offset = picks % rows_here
    sign = (1 - 2 * parity(source & me, 8)).astype(jnp.float32)
    column = offset // DEPTH
    odd = (column & 1).astype(jnp.float32)
    row = (column >> 1) * DEPTH + (offset % DEPTH)
    pieces = [
        sign * (1.0 - odd),
        sign * odd,
        (row & 127).astype(jnp.float32),
        (row >> 7).astype(jnp.float32),
    ]
    groups = picks.shape[0]
    up = lax.broadcasted_iota(jnp.int32, (LANES, 2 * LANES), 0)
    to = lax.broadcasted_iota(jnp.int32, (LANES, 2 * LANES), 1)
    upper = jnp.where((to >= LANES) | (up < to), 1.0, 0.0).astype(jnp.bfloat16)
    target = lax.broadcasted_iota(jnp.int32, (BLOCKS, LANES), 0)
    place = lax.broadcasted_iota(jnp.int32, (CAPACITY, LANES), 0)
    onehot = [jnp.where(rel[g:g + 1] == target, 1.0, 0.0) for g in range(groups)]
    counted = jnp.dot(
        jnp.concatenate(onehot, axis=0).astype(jnp.bfloat16),
        upper,
        preferred_element_type=jnp.float32,
    )
    base = jnp.zeros((BLOCKS, LANES), jnp.float32)
    total = jnp.zeros((len(pieces) * BLOCKS, LANES), jnp.float32)
    for g in range(groups):
        here = counted[g * BLOCKS:(g + 1) * BLOCKS]
        rank = jnp.sum(onehot[g] * (here[:, :LANES] + base), axis=0, keepdims=True)
        base = base + here[:, LANES:]
        at = jnp.where(rank.astype(jnp.int32) == place, 1.0, 0.0).astype(jnp.bfloat16)
        held = [onehot[g] * piece[g:g + 1] for piece in pieces]
        total = total + lax.dot_general(
            jnp.concatenate(held, axis=0).astype(jnp.bfloat16), at,
            (((1,), (1,)), ((), ())), preferred_element_type=jnp.float32,
        )
    weight_ref[...] = total[:2 * BLOCKS] * jnp.float32(2.0 ** -10)
    low = total[2 * BLOCKS:3 * BLOCKS].astype(jnp.int32)
    high = total[3 * BLOCKS:].astype(jnp.int32)
    listed_ref[:BLOCKS] = (high << 7) | low
    listed_ref[BLOCKS:] = base.astype(jnp.int32)


def take_rows(first, blocks, table, listed, rows):
    @pl.loop(0, blocks)
    def _(b):
        count = listed[BLOCKS + first + b, 0]
        for start in range(0, CAPACITY, STEP):
            @pl.when(count > start)
            def _():
                for at in range(start, start + STEP):
                    row = listed[first + b, at]
                    rows[pl.ds(b * CAPACITY + at, 1), :] = table[pl.ds(row, 1), :]


def turn_rows(first, blocks, rows, weight, out_ref):
    width = out_ref.shape[1]

    @pl.loop(0, blocks // 2)
    def _(pair):
        for b in (2 * pair, 2 * pair + 1):
            turned = rows[pl.ds(b * CAPACITY, CAPACITY), :].T
            even = weight[pl.ds(first + b, 1), :]
            odd = weight[pl.ds(BLOCKS + first + b, 1), :]
            zero = jnp.zeros((width, CAPACITY), jnp.float32)
            value = jnp.where(even != 0.0, turned[:width] * even, zero)
            out_ref[b] = jnp.where(odd != 0.0, turned[width:] * odd, value)


def transform_kernel(
    x_ref, bits_ref, picks_ref, owners_ref, send_ref, table, listed_ref, weight,
    x_buf, bits, picks, owners, signs, had, parts_a, parts_b, listed, rows,
    x_sem, small_sem, l_sem,
):
    width = x_ref.shape[0]
    rows_here = x_ref.shape[1]
    span = rows_here // CHUNKS
    me = lax.axis_index("row")

    small = [
        pltpu.make_async_copy(source, to, small_sem.at[n])
        for n, (source, to) in enumerate(
            ((picks_ref, picks), (owners_ref, owners), (bits_ref, bits))
        )
    ]
    def chunk(g):
        at = pl.multiple_of(g * span, span)
        return pltpu.make_async_copy(
            x_ref.at[:, pl.ds(at, span)], x_buf.at[g], x_sem.at[g]
        )

    for copy in small:
        copy.start()
    for g in range(AHEAD):
        chunk(g).start()

    i = lax.broadcasted_iota(jnp.int32, (DEPTH, DEPTH), 0)
    k = lax.broadcasted_iota(jnp.int32, (DEPTH, DEPTH), 1)
    matrix = (1 - 2 * parity(i & k, 8)).astype(jnp.float32).astype(jnp.bfloat16)
    had[:, :DEPTH] = matrix
    had[:, DEPTH:] = matrix
    small[0].wait()
    small[1].wait()
    list_samples(me, picks[...], owners[...], rows_here, listed_ref, weight)
    listing = pltpu.make_async_copy(listed_ref, listed, l_sem)
    listing.start()
    small[2].wait()
    signs[...] = (1 - 2 * bits[...]).astype(jnp.float32)

    def prepare(g, c, half, parts):
        values = []
        for j in range(INNER):
            at = j * DEPTH + half * LANES
            sign = signs[pl.ds(g * (span // LANES) + at // LANES, 1), :]
            values.append(x_buf[g, c:c + 16, at:at + LANES] * sign)
        for j, value in enumerate(butterflies(values)):
            high = value.astype(jnp.bfloat16)
            low = (value - high.astype(jnp.float32)).astype(jnp.bfloat16)
            at = slice(j * width + c, j * width + c + 16)
            parts[at, half * LANES:(half + 1) * LANES] = high
            parts[at, DEPTH + half * LANES:DEPTH + (half + 1) * LANES] = low

    def multiply(g, four, parts):
        made = lax.dot_general(
            had[...], parts[four * 4 * width:(four + 1) * 4 * width, :],
            (((1,), (1,)), ((), ())), preferred_element_type=jnp.float32,
        )
        at = (g * (INNER // 2) + four * 2) * DEPTH
        table[pl.ds(at, DEPTH), :] = made[:, :LANES]
        table[pl.ds(at + DEPTH, DEPTH), :] = made[:, LANES:]

    def stage(g, before, after):
        for four in range(4):
            if before is not None:
                multiply(g - 1, four, before)
            if after is not None:
                prepare(g, four * 16, 0, after)
                prepare(g, four * 16, 1, after)

    def wait(g):
        chunk(g).wait()

        @pl.when(g + AHEAD < CHUNKS)
        def _():
            chunk(g + AHEAD).start()

    wait(0)
    stage(0, None, parts_a)

    @pl.loop(0, CHUNKS // 2 - 1)
    def _(pair):
        wait(2 * pair + 1)
        stage(2 * pair + 1, parts_a, parts_b)
        wait(2 * pair + 2)
        stage(2 * pair + 2, parts_b, parts_a)

    wait(CHUNKS - 1)

    @pl.when(me < BLOCKS)
    def _():
        stage(CHUNKS - 1, parts_a, parts_b)

    @pl.when(me < BLOCKS)
    def _():
        stage(CHUNKS, parts_b, None)


    stretch = table.shape[0] // CHUNKS
    step = 32

    @pl.loop(0, stretch // step)
    def _(at):
        values = [table[pl.ds(g * stretch + at * step, step), :] for g in range(CHUNKS)]
        for g, value in enumerate(butterflies(values)):
            table[pl.ds(g * stretch + at * step, step), :] = value

    listing.wait()
    take_rows(BLOCKS // 2, BLOCKS // 2, table, listed, rows)
    turn_rows(BLOCKS // 2, BLOCKS // 2, rows, weight, send_ref)


def take_kernel(first, table, listed_ref, weight, out_ref, listed, rows, l_sem):
    blocks = out_ref.shape[0]
    copies = [
        pltpu.make_async_copy(
            listed_ref.at[at:at + BLOCKS // 2], listed.at[at:at + BLOCKS // 2], l_sem.at[n]
        )
        for n, at in enumerate((0, BLOCKS))
    ]
    for copy in copies:
        copy.start()
    for copy in copies:
        copy.wait()
    take_rows(first, blocks, table, listed, rows)
    turn_rows(first, blocks, rows, weight, out_ref)


VMEM = pl.BlockSpec(memory_space=pltpu.VMEM)
ANY = pl.BlockSpec(memory_space=pltpu.HBM)


def transform(design, bits, picks, owners):
    width, rows_here = design.shape
    f32, i32 = jnp.float32, jnp.int32
    return pl.pallas_call(
        transform_kernel,
        out_shape=(
            jax.ShapeDtypeStruct((BLOCKS // 2, width, CAPACITY), f32),
            jax.ShapeDtypeStruct((rows_here // 2, LANES), f32),
            jax.ShapeDtypeStruct((2 * BLOCKS, LANES), i32),
            jax.ShapeDtypeStruct((2 * BLOCKS, LANES), f32),
        ),
        in_specs=[ANY] * 4,
        out_specs=(VMEM,) * 4,
        scratch_shapes=[
            pltpu.VMEM((CHUNKS, width, rows_here // CHUNKS), f32),
            pltpu.VMEM(bits.shape, i32),
            pltpu.VMEM(picks.shape, i32),
            pltpu.VMEM(owners.shape, i32),
            pltpu.VMEM(bits.shape, f32),
            pltpu.VMEM((DEPTH, 2 * DEPTH), jnp.bfloat16),
            pltpu.VMEM((INNER * width, 2 * DEPTH), jnp.bfloat16),
            pltpu.VMEM((INNER * width, 2 * DEPTH), jnp.bfloat16),
            pltpu.SMEM((2 * BLOCKS, LANES), i32),
            pltpu.VMEM((BLOCKS // 2 * CAPACITY, LANES), f32),
            pltpu.SemaphoreType.DMA((CHUNKS,)),
            pltpu.SemaphoreType.DMA((3,)),
            pltpu.SemaphoreType.DMA,
        ],
        compiler_params=pltpu.CompilerParams(vmem_limit_bytes=24 << 20),
    )(*[
        pltpu.with_memory_space_constraint(a, pltpu.HBM)
        for a in (design, bits, picks, owners)
    ])


def take(first, blocks, width, table, listed, weight):
    return pl.pallas_call(
        functools.partial(take_kernel, first),
        out_shape=jax.ShapeDtypeStruct((blocks, width, CAPACITY), jnp.float32),
        in_specs=[VMEM] * 3,
        out_specs=VMEM,
        scratch_shapes=[
            pltpu.SMEM((2 * BLOCKS, LANES), jnp.int32),
            pltpu.VMEM((blocks * CAPACITY, LANES), jnp.float32),
            pltpu.SemaphoreType.DMA((2,)),
        ],
        compiler_params=pltpu.CompilerParams(vmem_limit_bytes=24 << 20),
        cost_estimate=pl.CostEstimate(
            flops=0, bytes_accessed=blocks << 18, transcendentals=0
        ),
    )(table, listed, weight)


def place(x, y, core):
    return (x * SIDE_Y + y) * 2 + core


def core_swap():
    return [(i, i ^ 1) for i in range(BLOCKS)]


def shift(step, first):
    pairs = []
    for x in range(SIDE_X):
        for y in range(SIDE_Y):
            for core in range(2):
                if (core == 0) == first:
                    to = place((x + step) % SIDE_X, y, core)
                else:
                    to = place(x, (y + step) % SIDE_Y, core)
                pairs.append((place(x, y, core), to))
    return pairs


def shards(design, sign_bits, picks, owners):
    width = design.shape[0]
    send, *made = transform(
        design,
        sign_bits.reshape(-1, LANES),
        picks.reshape(-1, LANES),
        owners.reshape(-1, LANES),
    )
    crossed = lax.ppermute(send, "row", core_swap())
    far = take(4, BLOCKS // 2 - 4, width, *made) + crossed[4:]
    moved = [
        lax.ppermute(far[step * 4 - 4:step * 4], "row", shift(step, True))
        for step in (1, 3, 2)
    ]
    own = take(0, 4, width, *made) + crossed[:4]
    for part in moved:
        own = own + part
    moved = [lax.ppermute(own[step], "row", shift(step, False)) for step in (1, 3, 2)]
    out = own[0]
    for part in moved:
        out = out + part
    return out


def solution(mesh):
    placed = (P("col", "row"), P("row"), P(), P())
    return jax.shard_map(
        shards, mesh=mesh, in_specs=placed, out_specs=P("col", "row"), check_vma=False
    )
```

```python
import functools

import jax
import jax.numpy as jnp
from jax import lax
from jax.experimental import pallas as pl
from jax.experimental.pallas import tpu as pltpu
from jax.sharding import PartitionSpec as P

LANES = 128
SIDE_X, SIDE_Y = 4, 4
CHUNKS = 8
INNER = 16
DEPTH = 256
CAPACITY = 128
STEP = 32
AHEAD = 3
BLOCKS = 32


def parity(value, bits):
    shift = 1
    while shift < bits:
        value = value ^ (value >> shift)
        shift = shift * 2
    return value & 1


def butterflies(values):
    half = 1
    values = list(values)
    while half < len(values):
        for start in range(0, len(values), 2 * half):
            for at in range(start, start + half):
                first, second = values[at], values[at + half]
                values[at], values[at + half] = first + second, first - second
        half = half * 2
    return values


def list_samples(me, picks, owners, rows_here, listed_ref, weight_ref):
    core, along_y, along_x = me & 1, (me >> 1) & 3, me >> 3
    owner_core = owners & 1
    rel_x = ((owners >> 3) - along_x) & 3
    rel_y = ((owners >> 1) - along_y) & 3
    first = jnp.where(owner_core == 0, rel_x, rel_y)
    second = jnp.where(owner_core == 0, rel_y, rel_x)
    rel = ((owner_core ^ core) << 4) | (first << 2) | second
    source = picks // rows_here
    offset = picks % rows_here
    sign = (1 - 2 * parity(source & me, 8)).astype(jnp.float32)
    column = offset // DEPTH
    odd = (column & 1).astype(jnp.float32)
    row = (column >> 1) * DEPTH + (offset % DEPTH)
    pieces = [
        sign * (1.0 - odd),
        sign * odd,
        (row & 127).astype(jnp.float32),
        (row >> 7).astype(jnp.float32),
    ]
    groups = picks.shape[0]
    up = lax.broadcasted_iota(jnp.int32, (LANES, 2 * LANES), 0)
    to = lax.broadcasted_iota(jnp.int32, (LANES, 2 * LANES), 1)
    upper = jnp.where((to >= LANES) | (up < to), 1.0, 0.0).astype(jnp.bfloat16)
    target = lax.broadcasted_iota(jnp.int32, (BLOCKS, LANES), 0)
    place = lax.broadcasted_iota(jnp.int32, (CAPACITY, LANES), 0)
    onehot = [jnp.where(rel[g:g + 1] == target, 1.0, 0.0) for g in range(groups)]
    counted = jnp.dot(
        jnp.concatenate(onehot, axis=0).astype(jnp.bfloat16),
        upper,
        preferred_element_type=jnp.float32,
    )
    base = jnp.zeros((BLOCKS, LANES), jnp.float32)
    total = jnp.zeros((len(pieces) * BLOCKS, LANES), jnp.float32)
    for g in range(groups):
        here = counted[g * BLOCKS:(g + 1) * BLOCKS]
        rank = jnp.sum(onehot[g] * (here[:, :LANES] + base), axis=0, keepdims=True)
        base = base + here[:, LANES:]
        at = jnp.where(rank.astype(jnp.int32) == place, 1.0, 0.0).astype(jnp.bfloat16)
        held = [onehot[g] * piece[g:g + 1] for piece in pieces]
        total = total + lax.dot_general(
            jnp.concatenate(held, axis=0).astype(jnp.bfloat16), at,
            (((1,), (1,)), ((), ())), preferred_element_type=jnp.float32,
        )
    weight_ref[...] = total[:2 * BLOCKS] * jnp.float32(2.0 ** -10)
    low = total[2 * BLOCKS:3 * BLOCKS].astype(jnp.int32)
    high = total[3 * BLOCKS:].astype(jnp.int32)
    listed_ref[:BLOCKS] = (high << 7) | low
    listed_ref[BLOCKS:] = base.astype(jnp.int32)


def take_rows(first, blocks, table, listed, rows):
    @pl.loop(0, blocks)
    def _(b):
        count = listed[BLOCKS + first + b, 0]
        for start in range(0, CAPACITY, STEP):
            @pl.when(count > start)
            def _():
                for at in range(start, start + STEP):
                    row = listed[first + b, at]
                    rows[pl.ds(b * CAPACITY + at, 1), :] = table[pl.ds(row, 1), :]


def turn_rows(first, blocks, rows, weight, out_ref):
    width = out_ref.shape[1]

    @pl.loop(0, blocks // 4)
    def _(group):
        for b in [4 * group + n for n in range(4)]:
            turned = rows[pl.ds(b * CAPACITY, CAPACITY), :].T
            even = weight[pl.ds(first + b, 1), :]
            odd = weight[pl.ds(BLOCKS + first + b, 1), :]
            zero = jnp.zeros((width, CAPACITY), jnp.float32)
            value = jnp.where(even != 0.0, turned[:width] * even, zero)
            out_ref[b] = jnp.where(odd != 0.0, turned[width:] * odd, value)


def transform_kernel(
    x_ref, bits_ref, picks_ref, owners_ref, send_ref, table, listed_ref, weight,
    x_buf, bits, picks, owners, signs, had, parts_a, parts_b, listed, rows,
    x_sem, small_sem, l_sem,
):
    width = x_ref.shape[0]
    rows_here = x_ref.shape[1]
    span = rows_here // CHUNKS
    me = lax.axis_index("row")

    small = [
        pltpu.make_async_copy(source, to, small_sem.at[n])
        for n, (source, to) in enumerate(
            ((picks_ref, picks), (owners_ref, owners), (bits_ref, bits))
        )
    ]
    def chunk(g):
        at = pl.multiple_of(g * span, span)
        return pltpu.make_async_copy(
            x_ref.at[:, pl.ds(at, span)], x_buf.at[g], x_sem.at[g]
        )

    for copy in small:
        copy.start()
    for g in range(AHEAD):
        chunk(g).start()

    i = lax.broadcasted_iota(jnp.int32, (DEPTH, DEPTH), 0)
    k = lax.broadcasted_iota(jnp.int32, (DEPTH, DEPTH), 1)
    matrix = (1 - 2 * parity(i & k, 8)).astype(jnp.float32).astype(jnp.bfloat16)
    had[:DEPTH, :DEPTH] = matrix
    had[:DEPTH, DEPTH:] = matrix
    small[0].wait()
    small[1].wait()
    list_samples(me, picks[...], owners[...], rows_here, listed_ref, weight)
    listing = pltpu.make_async_copy(listed_ref, listed, l_sem)
    listing.start()
    small[2].wait()
    signs[...] = (1 - 2 * bits[...]).astype(jnp.float32)

    def prepare(g, piece, parts):
        c, half = piece // 2 * 16, piece % 2
        values = []
        for j in range(INNER):
            at = j * DEPTH + half * LANES
            sign = signs[pl.ds(g * (span // LANES) + at // LANES, 1), :]
            values.append(x_buf[g, c:c + 16, at:at + LANES] * sign)
        for j, value in enumerate(butterflies(values[:8]) + butterflies(values[8:])):
            high = value.astype(jnp.bfloat16)
            low = (value - high.astype(jnp.float32)).astype(jnp.bfloat16)
            at = slice(j * width + c, j * width + c + 16)
            parts[at, half * LANES:(half + 1) * LANES] = high
            parts[at, DEPTH + half * LANES:DEPTH + (half + 1) * LANES] = low
        had[pl.ds(DEPTH + (g >> 8) * 16, 16), :LANES] = low
        x_buf[CHUNKS + (g >> 8), :16, :LANES] = low.astype(jnp.float32)

    def multiply(g, four, parts):
        made = lax.dot_general(
            had[:DEPTH], parts[four * 4 * width:(four + 1) * 4 * width, :],
            (((1,), (1,)), ((), ())), preferred_element_type=jnp.float32,
        )
        at = (g * (INNER // 2) + four * 2) * DEPTH
        table[pl.ds(at, DEPTH), :] = made[:, :LANES]
        table[pl.ds(at + DEPTH, DEPTH), :] = made[:, LANES:]

    def wait(g):
        chunk(g).wait()

        @pl.when(g + AHEAD < CHUNKS)
        def _():
            chunk(g + AHEAD).start()

    pieces = width // 8
    quads = INNER // 4

    def stage(g, before, after):
        for four in range(quads):
            if before is not None:
                multiply(g - 1, four, before)
            if after is not None:
                for piece in range(four * pieces // quads, (four + 1) * pieces // quads):
                    prepare(g, piece, after)

    wait(0)
    stage(0, None, parts_a)

    @pl.loop(0, CHUNKS // 2 - 1)
    def _(pair):
        wait(2 * pair + 1)
        stage(2 * pair + 1, parts_a, parts_b)
        wait(2 * pair + 2)
        stage(2 * pair + 2, parts_b, parts_a)

    wait(CHUNKS - 1)
    stage(CHUNKS - 1, parts_a, parts_b)
    stage(CHUNKS, parts_b, None)

    stretch = table.shape[0] // 16
    step = 16

    @pl.loop(0, stretch // step, unroll=2)
    def _(at):
        values = [table[pl.ds(g * stretch + at * step, step), :] for g in range(16)]
        for g, value in enumerate(butterflies(values)):
            table[pl.ds(g * stretch + at * step, step), :] = value

    listing.wait()
    take_rows(BLOCKS // 2, BLOCKS // 2, table, listed, rows)
    turn_rows(BLOCKS // 2, BLOCKS // 2, rows, weight, send_ref)


def take_kernel(first, table, listed_ref, weight, out_ref, listed, rows, l_sem):
    blocks = out_ref.shape[0]
    copies = [
        pltpu.make_async_copy(
            listed_ref.at[at:at + BLOCKS // 2], listed.at[at:at + BLOCKS // 2], l_sem.at[n]
        )
        for n, at in enumerate((0, BLOCKS))
    ]
    for copy in copies:
        copy.start()
    for copy in copies:
        copy.wait()
    take_rows(first, blocks, table, listed, rows)
    turn_rows(first, blocks, rows, weight, out_ref)


VMEM = pl.BlockSpec(memory_space=pltpu.VMEM)
ANY = pl.BlockSpec(memory_space=pltpu.HBM)


def transform(design, bits, picks, owners):
    width, rows_here = design.shape
    f32, i32 = jnp.float32, jnp.int32
    return pl.pallas_call(
        transform_kernel,
        out_shape=(
            jax.ShapeDtypeStruct((BLOCKS // 2, width, CAPACITY), f32),
            jax.ShapeDtypeStruct((rows_here // 2, LANES), f32),
            jax.ShapeDtypeStruct((2 * BLOCKS, LANES), i32),
            jax.ShapeDtypeStruct((2 * BLOCKS, LANES), f32),
        ),
        in_specs=[ANY] * 4,
        out_specs=(VMEM,) * 4,
        scratch_shapes=[
            pltpu.VMEM((CHUNKS + 1, width, rows_here // CHUNKS), f32),
            pltpu.VMEM(bits.shape, i32),
            pltpu.VMEM(picks.shape, i32),
            pltpu.VMEM(owners.shape, i32),
            pltpu.VMEM(bits.shape, f32),
            pltpu.VMEM((DEPTH + 16, 2 * DEPTH), jnp.bfloat16),
            pltpu.VMEM((INNER * width, 2 * DEPTH), jnp.bfloat16),
            pltpu.VMEM((INNER * width, 2 * DEPTH), jnp.bfloat16),
            pltpu.SMEM((2 * BLOCKS, LANES), i32),
            pltpu.VMEM((BLOCKS // 2 * CAPACITY, LANES), f32),
            pltpu.SemaphoreType.DMA((CHUNKS,)),
            pltpu.SemaphoreType.DMA((3,)),
            pltpu.SemaphoreType.DMA,
        ],
        compiler_params=pltpu.CompilerParams(vmem_limit_bytes=24 << 20),
    )(*[
        pltpu.with_memory_space_constraint(a, pltpu.HBM)
        for a in (design, bits, picks, owners)
    ])


def take(first, blocks, width, table, listed, weight):
    return pl.pallas_call(
        functools.partial(take_kernel, first),
        out_shape=jax.ShapeDtypeStruct((blocks, width, CAPACITY), jnp.float32),
        in_specs=[VMEM] * 3,
        out_specs=VMEM,
        scratch_shapes=[
            pltpu.SMEM((2 * BLOCKS, LANES), jnp.int32),
            pltpu.VMEM((blocks * CAPACITY, LANES), jnp.float32),
            pltpu.SemaphoreType.DMA((2,)),
        ],
        compiler_params=pltpu.CompilerParams(vmem_limit_bytes=24 << 20),
        cost_estimate=pl.CostEstimate(
            flops=0, bytes_accessed=blocks << 18, transcendentals=0
        ),
    )(table, listed, weight)


def place(x, y, core):
    return (x * SIDE_Y + y) * 2 + core


def core_swap():
    return [(i, i ^ 1) for i in range(BLOCKS)]


def shift(step, first):
    pairs = []
    for x in range(SIDE_X):
        for y in range(SIDE_Y):
            for core in range(2):
                if (core == 0) == first:
                    to = place((x + step) % SIDE_X, y, core)
                else:
                    to = place(x, (y + step) % SIDE_Y, core)
                pairs.append((place(x, y, core), to))
    return pairs


def shards(design, sign_bits, picks, owners):
    width = design.shape[0]
    send, *made = transform(
        design,
        sign_bits.reshape(-1, LANES),
        picks.reshape(-1, LANES),
        owners.reshape(-1, LANES),
    )
    crossed = lax.ppermute(send, "row", core_swap())
    far = take(4, BLOCKS // 2 - 4, width, *made) + crossed[4:]
    moved = [
        lax.ppermute(far[step * 4 - 4:step * 4], "row", shift(step, True))
        for step in (1, 3, 2)
    ]
    own = take(0, 4, width, *made) + crossed[:4]
    for part in moved:
        own = own + part
    moved = [lax.ppermute(own[step], "row", shift(step, False)) for step in (1, 3, 2)]
    out = own[0]
    for part in moved:
        out = out + part
    return out


def solution(mesh):
    placed = (P("col", "row"), P("row"), P(), P())
    return jax.shard_map(
        shards, mesh=mesh, in_specs=placed, out_specs=P("col", "row"), check_vma=False
    )
```

```python
import functools

import jax
import jax.numpy as jnp
from jax import lax
from jax.experimental import pallas as pl
from jax.experimental.pallas import tpu as pltpu
from jax.sharding import PartitionSpec as P

LANES = 128
SIDE_X, SIDE_Y = 4, 4
CHUNKS = 8
INNER = 16
DEPTH = 256
CAPACITY = 128
STEP = 64
AHEAD = 3
BLOCKS = 32


def parity(value, bits):
    shift = 1
    while shift < bits:
        value = value ^ (value >> shift)
        shift = shift * 2
    return value & 1


def butterflies(values):
    half = 1
    values = list(values)
    while half < len(values):
        for start in range(0, len(values), 2 * half):
            for at in range(start, start + half):
                first, second = values[at], values[at + half]
                values[at], values[at + half] = first + second, first - second
        half = half * 2
    return values


def list_samples(me, picks, owners, rows_here, listed_ref, weight_ref):
    core, along_y, along_x = me & 1, (me >> 1) & 3, me >> 3
    owner_core = owners & 1
    rel_x = ((owners >> 3) - along_x) & 3
    rel_y = ((owners >> 1) - along_y) & 3
    first = jnp.where(owner_core == 0, rel_x, rel_y)
    second = jnp.where(owner_core == 0, rel_y, rel_x)
    rel = ((owner_core ^ core) << 4) | (first << 2) | second
    source = picks // rows_here
    offset = picks % rows_here
    sign = (1 - 2 * parity(source & me, 8)).astype(jnp.float32)
    column = offset // DEPTH
    odd = (column & 1).astype(jnp.float32)
    row = (column >> 1) * DEPTH + (offset % DEPTH)
    pieces = [
        sign * (1.0 - odd),
        sign * odd,
        (row & 127).astype(jnp.float32),
        (row >> 7).astype(jnp.float32),
    ]
    groups = picks.shape[0]
    up = lax.broadcasted_iota(jnp.int32, (LANES, 2 * LANES), 0)
    to = lax.broadcasted_iota(jnp.int32, (LANES, 2 * LANES), 1)
    upper = jnp.where((to >= LANES) | (up < to), 1.0, 0.0).astype(jnp.bfloat16)
    target = lax.broadcasted_iota(jnp.int32, (BLOCKS, LANES), 0)
    place = lax.broadcasted_iota(jnp.int32, (CAPACITY, LANES), 0)
    onehot = [jnp.where(rel[g:g + 1] == target, 1.0, 0.0) for g in range(groups)]
    counted = jnp.dot(
        jnp.concatenate(onehot, axis=0).astype(jnp.bfloat16),
        upper,
        preferred_element_type=jnp.float32,
    )
    base = jnp.zeros((BLOCKS, LANES), jnp.float32)
    total = jnp.zeros((len(pieces) * BLOCKS, LANES), jnp.float32)
    for g in range(groups):
        here = counted[g * BLOCKS:(g + 1) * BLOCKS]
        rank = jnp.sum(onehot[g] * (here[:, :LANES] + base), axis=0, keepdims=True)
        base = base + here[:, LANES:]
        at = jnp.where(rank.astype(jnp.int32) == place, 1.0, 0.0).astype(jnp.bfloat16)
        held = [onehot[g] * piece[g:g + 1] for piece in pieces]
        total = total + lax.dot_general(
            jnp.concatenate(held, axis=0).astype(jnp.bfloat16), at,
            (((1,), (1,)), ((), ())), preferred_element_type=jnp.float32,
        )
    weight_ref[...] = total[:2 * BLOCKS] * jnp.float32(2.0 ** -10)
    low = total[2 * BLOCKS:3 * BLOCKS].astype(jnp.int32)
    high = total[3 * BLOCKS:].astype(jnp.int32)
    listed_ref[:BLOCKS] = (high << 7) | low
    listed_ref[BLOCKS:] = base.astype(jnp.int32)


def take_rows(first, blocks, table, listed, rows):
    @pl.loop(0, blocks)
    def _(b):
        count = listed[BLOCKS + first + b, 0]
        for start in range(0, CAPACITY, STEP):
            @pl.when(count > start)
            def _():
                for at in range(start, start + STEP):
                    row = listed[first + b, at]
                    rows[pl.ds(b * CAPACITY + at, 1), :] = table[pl.ds(row, 1), :]


def turn_rows(first, blocks, rows, weight, out_ref):
    width = out_ref.shape[1]

    size = max(n for n in (4, 6, 8) if blocks % n == 0)

    @pl.loop(0, blocks // size)
    def _(group):
        for b in [size * group + n for n in range(size)]:
            turned = rows[pl.ds(b * CAPACITY, CAPACITY), :].T
            even = weight[pl.ds(first + b, 1), :]
            odd = weight[pl.ds(BLOCKS + first + b, 1), :]
            zero = jnp.zeros((width, CAPACITY), jnp.float32)
            value = jnp.where(even != 0.0, turned[:width] * even, zero)
            out_ref[b] = jnp.where(odd != 0.0, turned[width:] * odd, value)


def transform_kernel(
    x_ref, bits_ref, picks_ref, owners_ref, send_ref, table, listed_ref, weight,
    x_buf, bits, picks, owners, signs, had, parts_a, parts_b, listed, rows,
    x_sem, small_sem, l_sem,
):
    width = x_ref.shape[0]
    rows_here = x_ref.shape[1]
    span = rows_here // CHUNKS
    me = lax.axis_index("row")

    small = [
        pltpu.make_async_copy(source, to, small_sem.at[n])
        for n, (source, to) in enumerate(
            ((picks_ref, picks), (owners_ref, owners), (bits_ref, bits))
        )
    ]
    def chunk(g):
        at = pl.multiple_of(g * span, span)
        return pltpu.make_async_copy(
            x_ref.at[:, pl.ds(at, span)], x_buf.at[g], x_sem.at[g]
        )

    for copy in small:
        copy.start()
    for g in range(AHEAD):
        chunk(g).start()

    i = lax.broadcasted_iota(jnp.int32, (DEPTH, DEPTH), 0)
    k = lax.broadcasted_iota(jnp.int32, (DEPTH, DEPTH), 1)
    matrix = (1 - 2 * parity(i & k, 8)).astype(jnp.float32).astype(jnp.bfloat16)
    had[:DEPTH, :DEPTH] = matrix
    had[:DEPTH, DEPTH:] = matrix
    small[0].wait()
    small[1].wait()
    list_samples(me, picks[...], owners[...], rows_here, listed_ref, weight)
    listing = pltpu.make_async_copy(listed_ref, listed, l_sem)
    listing.start()
    small[2].wait()
    signs[...] = (1 - 2 * bits[...]).astype(jnp.float32)

    def prepare(g, piece, parts):
        c, half = piece // 2 * 16, piece % 2
        values = []
        for j in range(INNER):
            at = j * DEPTH + half * LANES
            sign = signs[pl.ds(g * (span // LANES) + at // LANES, 1), :]
            values.append(x_buf[g, c:c + 16, at:at + LANES] * sign)
        for j, value in enumerate(butterflies(values[:8]) + butterflies(values[8:])):
            high = value.astype(jnp.bfloat16)
            low = (value - high.astype(jnp.float32)).astype(jnp.bfloat16)
            at = slice(j * width + c, j * width + c + 16)
            parts[at, half * LANES:(half + 1) * LANES] = high
            parts[at, DEPTH + half * LANES:DEPTH + (half + 1) * LANES] = low
        if isinstance(g, int) and g == 0:
            return
        had[pl.ds(DEPTH + (g >> 8) * 16, 16), :LANES] = low
        x_buf[CHUNKS + (g >> 8), :16, :LANES] = low.astype(jnp.float32)

    def multiply(g, four, parts):
        made = lax.dot_general(
            had[:DEPTH], parts[four * 4 * width:(four + 1) * 4 * width, :],
            (((1,), (1,)), ((), ())), preferred_element_type=jnp.float32,
        )
        at = (g * (INNER // 2) + four * 2) * DEPTH
        table[pl.ds(at, DEPTH), :] = made[:, :LANES]
        table[pl.ds(at + DEPTH, DEPTH), :] = made[:, LANES:]

    def wait(g):
        chunk(g).wait()

        @pl.when(g + AHEAD < CHUNKS)
        def _():
            chunk(g + AHEAD).start()

    pieces = width // 8
    quads = INNER // 4

    def stage(g, before, after):
        for four in range(quads):
            if before is not None:
                multiply(g - 1, four, before)
            if after is not None:
                for piece in range(four * pieces // quads, (four + 1) * pieces // quads):
                    prepare(g, piece, after)

    wait(0)
    stage(0, None, parts_a)

    @pl.loop(0, CHUNKS // 2 - 1)
    def _(pair):
        wait(2 * pair + 1)
        stage(2 * pair + 1, parts_a, parts_b)
        wait(2 * pair + 2)
        stage(2 * pair + 2, parts_b, parts_a)

    wait(CHUNKS - 1)
    stage(CHUNKS - 1, parts_a, parts_b)
    stage(CHUNKS, parts_b, None)

    stretch = table.shape[0] // 16
    step = 16

    @pl.loop(0, stretch // step, unroll=2)
    def _(at):
        values = [table[pl.ds(g * stretch + at * step, step), :] for g in range(16)]
        for g, value in enumerate(butterflies(values)):
            table[pl.ds(g * stretch + at * step, step), :] = value

    listing.wait()
    take_rows(BLOCKS // 2, BLOCKS // 2, table, listed, rows)
    turn_rows(BLOCKS // 2, BLOCKS // 2, rows, weight, send_ref)


def take_kernel(first, table, listed_ref, weight, out_ref, listed, rows, l_sem):
    blocks = out_ref.shape[0]
    copies = [
        pltpu.make_async_copy(
            listed_ref.at[at:at + BLOCKS // 2], listed.at[at:at + BLOCKS // 2], l_sem.at[n]
        )
        for n, at in enumerate((0, BLOCKS))
    ]
    for copy in copies:
        copy.start()
    for copy in copies:
        copy.wait()
    take_rows(first, blocks, table, listed, rows)
    turn_rows(first, blocks, rows, weight, out_ref)


VMEM = pl.BlockSpec(memory_space=pltpu.VMEM)
ANY = pl.BlockSpec(memory_space=pltpu.HBM)


def transform(design, bits, picks, owners):
    width, rows_here = design.shape
    f32, i32 = jnp.float32, jnp.int32
    return pl.pallas_call(
        transform_kernel,
        out_shape=(
            jax.ShapeDtypeStruct((BLOCKS // 2, width, CAPACITY), f32),
            jax.ShapeDtypeStruct((rows_here // 2, LANES), f32),
            jax.ShapeDtypeStruct((2 * BLOCKS, LANES), i32),
            jax.ShapeDtypeStruct((2 * BLOCKS, LANES), f32),
        ),
        in_specs=[ANY] * 4,
        out_specs=(VMEM,) * 4,
        scratch_shapes=[
            pltpu.VMEM((CHUNKS + 1, width, rows_here // CHUNKS), f32),
            pltpu.VMEM(bits.shape, i32),
            pltpu.VMEM(picks.shape, i32),
            pltpu.VMEM(owners.shape, i32),
            pltpu.VMEM(bits.shape, f32),
            pltpu.VMEM((DEPTH + 16, 2 * DEPTH), jnp.bfloat16),
            pltpu.VMEM((INNER * width, 2 * DEPTH), jnp.bfloat16),
            pltpu.VMEM((INNER * width, 2 * DEPTH), jnp.bfloat16),
            pltpu.SMEM((2 * BLOCKS, LANES), i32),
            pltpu.VMEM((BLOCKS // 2 * CAPACITY, LANES), f32),
            pltpu.SemaphoreType.DMA((CHUNKS,)),
            pltpu.SemaphoreType.DMA((3,)),
            pltpu.SemaphoreType.DMA,
        ],
        compiler_params=pltpu.CompilerParams(vmem_limit_bytes=24 << 20),
    )(*[
        pltpu.with_memory_space_constraint(a, pltpu.HBM)
        for a in (design, bits, picks, owners)
    ])


def take(first, blocks, width, table, listed, weight):
    return pl.pallas_call(
        functools.partial(take_kernel, first),
        out_shape=jax.ShapeDtypeStruct((blocks, width, CAPACITY), jnp.float32),
        in_specs=[VMEM] * 3,
        out_specs=VMEM,
        scratch_shapes=[
            pltpu.SMEM((2 * BLOCKS, LANES), jnp.int32),
            pltpu.VMEM((blocks * CAPACITY, LANES), jnp.float32),
            pltpu.SemaphoreType.DMA((2,)),
        ],
        compiler_params=pltpu.CompilerParams(vmem_limit_bytes=24 << 20),
        cost_estimate=pl.CostEstimate(
            flops=0, bytes_accessed=blocks << 18, transcendentals=0
        ),
    )(table, listed, weight)


def place(x, y, core):
    return (x * SIDE_Y + y) * 2 + core


def core_swap():
    return [(i, i ^ 1) for i in range(BLOCKS)]


def shift(step, first):
    pairs = []
    for x in range(SIDE_X):
        for y in range(SIDE_Y):
            for core in range(2):
                if (core == 0) == first:
                    to = place((x + step) % SIDE_X, y, core)
                else:
                    to = place(x, (y + step) % SIDE_Y, core)
                pairs.append((place(x, y, core), to))
    return pairs


def shards(design, sign_bits, picks, owners):
    width = design.shape[0]
    send, *made = transform(
        design,
        sign_bits.reshape(-1, LANES),
        picks.reshape(-1, LANES),
        owners.reshape(-1, LANES),
    )
    crossed = lax.ppermute(send, "row", core_swap())
    far = take(4, BLOCKS // 2 - 4, width, *made) + crossed[4:]
    moved = [
        lax.ppermute(far[step * 4 - 4:step * 4], "row", shift(step, True))
        for step in (1, 3, 2)
    ]
    own = take(0, 4, width, *made) + crossed[:4]
    for part in moved:
        own = own + part
    moved = [lax.ppermute(own[step], "row", shift(step, False)) for step in (1, 3, 2)]
    out = own[0]
    for part in moved:
        out = out + part
    return out


def solution(mesh):
    placed = (P("col", "row"), P("row"), P(), P())
    return jax.shard_map(
        shards, mesh=mesh, in_specs=placed, out_specs=P("col", "row"), check_vma=False
    )
```

```python
import functools

import jax
import jax.numpy as jnp
from jax import lax
from jax.experimental import pallas as pl
from jax.experimental.pallas import tpu as pltpu
from jax.sharding import PartitionSpec as P

LANES = 128
SIDE_X, SIDE_Y = 4, 4
CHUNKS = 8
INNER = 16
DEPTH = 256
CAPACITY = 128
STEP = 64
AHEAD = 3
BLOCKS = 32


def parity(value, bits):
    shift = 1
    while shift < bits:
        value = value ^ (value >> shift)
        shift = shift * 2
    return value & 1


def butterflies(values):
    half = 1
    values = list(values)
    while half < len(values):
        for start in range(0, len(values), 2 * half):
            for at in range(start, start + half):
                first, second = values[at], values[at + half]
                values[at], values[at + half] = first + second, first - second
        half = half * 2
    return values


def list_samples(me, picks, owners, rows_here, listed_ref, weight_ref):
    core, along_y, along_x = me & 1, (me >> 1) & 3, me >> 3
    owner_core = owners & 1
    rel_x = ((owners >> 3) - along_x) & 3
    rel_y = ((owners >> 1) - along_y) & 3
    first = jnp.where(owner_core == 0, rel_x, rel_y)
    second = jnp.where(owner_core == 0, rel_y, rel_x)
    rel = ((owner_core ^ core) << 4) | (first << 2) | second
    source = picks // rows_here
    offset = picks % rows_here
    sign = (1 - 2 * parity(source & me, 8)).astype(jnp.float32)
    column = offset // DEPTH
    odd = (column & 1).astype(jnp.float32)
    row = (column >> 1) * DEPTH + (offset % DEPTH)
    pieces = [
        sign * (1.0 - odd),
        sign * odd,
        (row & 127).astype(jnp.float32),
        (row >> 7).astype(jnp.float32),
    ]
    groups = picks.shape[0]
    up = lax.broadcasted_iota(jnp.int32, (LANES, 2 * LANES), 0)
    to = lax.broadcasted_iota(jnp.int32, (LANES, 2 * LANES), 1)
    upper = jnp.where((to >= LANES) | (up < to), 1.0, 0.0).astype(jnp.bfloat16)
    target = lax.broadcasted_iota(jnp.int32, (BLOCKS, LANES), 0)
    place = lax.broadcasted_iota(jnp.int32, (CAPACITY, LANES), 0)
    onehot = [jnp.where(rel[g:g + 1] == target, 1.0, 0.0) for g in range(groups)]
    counted = jnp.dot(
        jnp.concatenate(onehot, axis=0).astype(jnp.bfloat16),
        upper,
        preferred_element_type=jnp.float32,
    )
    base = jnp.zeros((BLOCKS, LANES), jnp.float32)
    total = jnp.zeros((len(pieces) * BLOCKS, LANES), jnp.float32)
    for g in range(groups):
        here = counted[g * BLOCKS:(g + 1) * BLOCKS]
        rank = jnp.sum(onehot[g] * (here[:, :LANES] + base), axis=0, keepdims=True)
        base = base + here[:, LANES:]
        at = jnp.where(rank.astype(jnp.int32) == place, 1.0, 0.0).astype(jnp.bfloat16)
        held = [onehot[g] * piece[g:g + 1] for piece in pieces]
        total = total + lax.dot_general(
            jnp.concatenate(held, axis=0).astype(jnp.bfloat16), at,
            (((1,), (1,)), ((), ())), preferred_element_type=jnp.float32,
        )
    weight_ref[...] = total[:2 * BLOCKS] * jnp.float32(2.0 ** -10)
    low = total[2 * BLOCKS:3 * BLOCKS].astype(jnp.int32)
    high = total[3 * BLOCKS:].astype(jnp.int32)
    listed_ref[:BLOCKS] = (high << 7) | low
    listed_ref[BLOCKS:] = base.astype(jnp.int32)


def take_rows(first, blocks, table, listed, rows):
    @pl.loop(0, blocks)
    def _(b):
        count = listed[BLOCKS + first + b, 0]
        for start in range(0, CAPACITY, STEP):
            @pl.when(count > start)
            def _():
                for at in range(start, start + STEP):
                    row = listed[first + b, at]
                    rows[pl.ds(b * CAPACITY + at, 1), :] = table[pl.ds(row, 1), :]


def turn_rows(first, blocks, rows, weight, out_ref):
    width = out_ref.shape[1]

    size = max(n for n in (4, 6, 8) if blocks % n == 0)

    @pl.loop(0, blocks // size)
    def _(group):
        for b in [size * group + n for n in range(size)]:
            turned = rows[pl.ds(b * CAPACITY, CAPACITY), :].T
            even = weight[pl.ds(first + b, 1), :]
            odd = weight[pl.ds(BLOCKS + first + b, 1), :]
            zero = jnp.zeros((width, CAPACITY), jnp.float32)
            value = jnp.where(even != 0.0, turned[:width] * even, zero)
            out_ref[b] = jnp.where(odd != 0.0, turned[width:] * odd, value)


def transform_kernel(
    x_ref, bits_ref, picks_ref, owners_ref, send_ref, table, listed_ref, weight,
    x_buf, bits, picks, owners, signs, had, parts_a, parts_b, listed, rows,
    x_sem, small_sem, l_sem,
):
    width = x_ref.shape[0]
    rows_here = x_ref.shape[1]
    span = rows_here // CHUNKS
    me = lax.axis_index("row")

    small = [
        pltpu.make_async_copy(source, to, small_sem.at[n])
        for n, (source, to) in enumerate(
            ((picks_ref, picks), (owners_ref, owners), (bits_ref, bits))
        )
    ]
    def chunk(g):
        at = pl.multiple_of(g * span, span)
        return pltpu.make_async_copy(
            x_ref.at[:, pl.ds(at, span)], x_buf.at[g], x_sem.at[g]
        )

    for copy in small:
        copy.start()
    for g in range(AHEAD):
        chunk(g).start()

    i = lax.broadcasted_iota(jnp.int32, (DEPTH, DEPTH), 0)
    k = lax.broadcasted_iota(jnp.int32, (DEPTH, DEPTH), 1)
    matrix = (1 - 2 * parity(i & k, 8)).astype(jnp.float32).astype(jnp.bfloat16)
    had[:DEPTH, :DEPTH] = matrix
    had[:DEPTH, DEPTH:] = matrix
    small[0].wait()
    small[1].wait()
    list_samples(me, picks[...], owners[...], rows_here, listed_ref, weight)
    listing = pltpu.make_async_copy(listed_ref, listed, l_sem)
    listing.start()
    small[2].wait()
    signs[...] = (1 - 2 * bits[...]).astype(jnp.float32)

    def prepare(g, piece, parts):
        c, half = piece // 2 * 16, piece % 2
        values = []
        for j in range(INNER):
            at = j * DEPTH + half * LANES
            sign = signs[pl.ds(g * (span // LANES) + at // LANES, 1), :]
            values.append(x_buf[g, c:c + 16, at:at + LANES] * sign)
        for j, value in enumerate(butterflies(values[:8]) + butterflies(values[8:])):
            high = value.astype(jnp.bfloat16)
            low = (value - high.astype(jnp.float32)).astype(jnp.bfloat16)
            at = slice(j * width + c, j * width + c + 16)
            parts[at, half * LANES:(half + 1) * LANES] = high
            parts[at, DEPTH + half * LANES:DEPTH + (half + 1) * LANES] = low
        if isinstance(g, int) and g == 0:
            return
        had[pl.ds(DEPTH + (g >> 8) * 16, 16), :LANES] = low
        x_buf[CHUNKS + (g >> 8), :16, :LANES] = low.astype(jnp.float32)

    def multiply(g, four, parts):
        made = lax.dot_general(
            had[:DEPTH], parts[four * 4 * width:(four + 1) * 4 * width, :],
            (((1,), (1,)), ((), ())), preferred_element_type=jnp.float32,
        )
        at = (g * (INNER // 2) + four * 2) * DEPTH
        table[pl.ds(at, DEPTH), :] = made[:, :LANES]
        table[pl.ds(at + DEPTH, DEPTH), :] = made[:, LANES:]

    def wait(g):
        chunk(g).wait()

        @pl.when(g + AHEAD < CHUNKS)
        def _():
            chunk(g + AHEAD).start()

    pieces = width // 8
    quads = INNER // 4

    def stage(g, before, after):
        for four in range(quads):
            if before is not None:
                multiply(g - 1, four, before)
            if after is not None:
                for piece in range(four * pieces // quads, (four + 1) * pieces // quads):
                    prepare(g, piece, after)

    wait(0)
    stage(0, None, parts_a)

    @pl.loop(0, CHUNKS // 2 - 1)
    def _(pair):
        wait(2 * pair + 1)
        stage(2 * pair + 1, parts_a, parts_b)
        wait(2 * pair + 2)
        stage(2 * pair + 2, parts_b, parts_a)

    wait(CHUNKS - 1)
    stage(CHUNKS - 1, parts_a, parts_b)
    stage(CHUNKS, parts_b, None)

    stretch = table.shape[0] // 16
    step = 16

    @pl.loop(0, stretch // step, unroll=4)
    def _(at):
        values = [table[pl.ds(g * stretch + at * step, step), :] for g in range(16)]
        for g, value in enumerate(butterflies(values)):
            table[pl.ds(g * stretch + at * step, step), :] = value

    listing.wait()
    take_rows(BLOCKS // 2, BLOCKS // 2, table, listed, rows)
    turn_rows(BLOCKS // 2, BLOCKS // 2, rows, weight, send_ref)


def take_kernel(first, table, listed_ref, weight, out_ref, listed, rows, l_sem):
    blocks = out_ref.shape[0]
    copies = [
        pltpu.make_async_copy(
            listed_ref.at[at:at + BLOCKS // 2], listed.at[at:at + BLOCKS // 2], l_sem.at[n]
        )
        for n, at in enumerate((0, BLOCKS))
    ]
    for copy in copies:
        copy.start()
    for copy in copies:
        copy.wait()
    take_rows(first, blocks, table, listed, rows)
    turn_rows(first, blocks, rows, weight, out_ref)


VMEM = pl.BlockSpec(memory_space=pltpu.VMEM)
ANY = pl.BlockSpec(memory_space=pltpu.HBM)


def transform(design, bits, picks, owners):
    width, rows_here = design.shape
    f32, i32 = jnp.float32, jnp.int32
    return pl.pallas_call(
        transform_kernel,
        out_shape=(
            jax.ShapeDtypeStruct((BLOCKS // 2, width, CAPACITY), f32),
            jax.ShapeDtypeStruct((rows_here // 2, LANES), f32),
            jax.ShapeDtypeStruct((2 * BLOCKS, LANES), i32),
            jax.ShapeDtypeStruct((2 * BLOCKS, LANES), f32),
        ),
        in_specs=[ANY] * 4,
        out_specs=(VMEM,) * 4,
        scratch_shapes=[
            pltpu.VMEM((CHUNKS + 1, width, rows_here // CHUNKS), f32),
            pltpu.VMEM(bits.shape, i32),
            pltpu.VMEM(picks.shape, i32),
            pltpu.VMEM(owners.shape, i32),
            pltpu.VMEM(bits.shape, f32),
            pltpu.VMEM((DEPTH + 16, 2 * DEPTH), jnp.bfloat16),
            pltpu.VMEM((INNER * width, 2 * DEPTH), jnp.bfloat16),
            pltpu.VMEM((INNER * width, 2 * DEPTH), jnp.bfloat16),
            pltpu.SMEM((2 * BLOCKS, LANES), i32),
            pltpu.VMEM((BLOCKS // 2 * CAPACITY, LANES), f32),
            pltpu.SemaphoreType.DMA((CHUNKS,)),
            pltpu.SemaphoreType.DMA((3,)),
            pltpu.SemaphoreType.DMA,
        ],
        compiler_params=pltpu.CompilerParams(vmem_limit_bytes=24 << 20),
    )(*[
        pltpu.with_memory_space_constraint(a, pltpu.HBM)
        for a in (design, bits, picks, owners)
    ])


def take(first, blocks, width, table, listed, weight):
    return pl.pallas_call(
        functools.partial(take_kernel, first),
        out_shape=jax.ShapeDtypeStruct((blocks, width, CAPACITY), jnp.float32),
        in_specs=[VMEM] * 3,
        out_specs=VMEM,
        scratch_shapes=[
            pltpu.SMEM((2 * BLOCKS, LANES), jnp.int32),
            pltpu.VMEM((blocks * CAPACITY, LANES), jnp.float32),
            pltpu.SemaphoreType.DMA((2,)),
        ],
        compiler_params=pltpu.CompilerParams(vmem_limit_bytes=24 << 20),
        cost_estimate=pl.CostEstimate(
            flops=0, bytes_accessed=blocks << 18, transcendentals=0
        ),
    )(table, listed, weight)


def place(x, y, core):
    return (x * SIDE_Y + y) * 2 + core


def core_swap():
    return [(i, i ^ 1) for i in range(BLOCKS)]


def shift(step, first):
    pairs = []
    for x in range(SIDE_X):
        for y in range(SIDE_Y):
            for core in range(2):
                if (core == 0) == first:
                    to = place((x + step) % SIDE_X, y, core)
                else:
                    to = place(x, (y + step) % SIDE_Y, core)
                pairs.append((place(x, y, core), to))
    return pairs


def shards(design, sign_bits, picks, owners):
    width = design.shape[0]
    send, *made = transform(
        design,
        sign_bits.reshape(-1, LANES),
        picks.reshape(-1, LANES),
        owners.reshape(-1, LANES),
    )
    crossed = lax.ppermute(send, "row", core_swap())
    far = take(4, BLOCKS // 2 - 4, width, *made) + crossed[4:]
    moved = [
        lax.ppermute(far[step * 4 - 4:step * 4], "row", shift(step, True))
        for step in (1, 3, 2)
    ]
    own = take(0, 4, width, *made) + crossed[:4]
    for part in moved:
        own = own + part
    moved = [lax.ppermute(own[step], "row", shift(step, False)) for step in (1, 3, 2)]
    out = own[0]
    for part in moved:
        out = out + part
    return out


def solution(mesh):
    placed = (P("col", "row"), P("row"), P(), P())
    return jax.shard_map(
        shards, mesh=mesh, in_specs=placed, out_specs=P("col", "row"), check_vma=False
    )
```
